256 devices in a mesh: grp: 16 (over x, y), sp: 16 (over z, core).
Axes of the slice: x: 4, y: 4, z: 8, core: 2. Of those that a mesh axis runs over, the one named last changes fastest.
Arguments:
- query_in: bfloat16 [32768, 4096], P(('grp', 'sp')), may hold values from -200 to 200, as said below
- key_in: bfloat16 [32768, 4096], P(('grp', 'sp')), may hold values from -200 to 200, as said below
- value_in: bfloat16 [32768, 4096], P(('grp', 'sp')), may hold values from -6 to 6
- out_cotangent: bfloat16 [32768, 4096], P(('grp', 'sp')), may hold values from -6 to 6
- query_gain: float32 [4096], replicated, may hold values from 0.8 to 2.5
- key_gain: float32 [4096], replicated, may hold values from 0.8 to 2.5
- frames: int32 [16, 4], P('grp'), may hold values from 1 to 21, 32 in all within a row
- slab_group: int32 [16, 16, 16], P('grp', 'sp'), may hold values from 0 to 15, each once within a row
Outputs:
- attn_out: bfloat16 [32768, 4096], P(('grp', 'sp'))
- grad_q: bfloat16 [32768, 4096], P(('grp', 'sp'))
- grad_k: bfloat16 [32768, 4096], P(('grp', 'sp'))
- grad_v: bfloat16 [32768, 4096], P(('grp', 'sp'))
The draws below stay inside these ranges and needn't reach their ends.
Inputs may be any that keep to these rules, and one draw needn't show every extreme that they name: Each row lists the latent frames of the 4 videos of one group; a row sums to 32 and its largest entry is exactly 21. `slab_group`: for each device's block, the 8-token slabs go one to each group. `query_in`: real values. `key_in`: real values.
All inputs are finite; a program needn't handle non-finite values.
Results may differ from the reference program's by a relative error of at most 0.04.
The reference program's roundings to bfloat16 on the way count: a program that leaves them out, or rounds other values in their place, can miss the bound.
Values may be sent and summed in bfloat16 or wider, within the bound.
No kernel may reach another device: no remote copies, remote signals or barrier semaphores. Data moves between devices by JAX's collectives and lax.ppermute only.
A program may use at most 128 MiB of HBM per device.

```python
import math
import jax
import jax.numpy as jnp
import numpy as np
from jax import lax

HDIM = 128
TOK_FRAME = 64
HEADS = 32
WIDTH = 4096
S_GRP = 2048
TOKENS = 32768
SLAB = 8
FRAMES_GRP = 32
NVID = 4
MOSTF = 21
N_GRP = 16
N_SP = 16


def rough_field(key, lowest, highest):
    column_scale = jnp.exp(jax.random.uniform(jax.random.fold_in(key, 1), (1, WIDTH), jnp.float32, math.log(lowest), math.log(highest)))
    values = jax.random.normal(jax.random.fold_in(key, 2), (TOKENS, WIDTH), jnp.float32)
    return (values, column_scale)


def draw_query_in(key, part):
    key = jax.random.fold_in(key, 7)
    values, column_scale = rough_field(key, 0.3, 3.0)
    values = values * column_scale
    return jnp.clip(values, -200.0, 200.0).astype(jnp.bfloat16)


def draw_key_in(key, part):
    key = jax.random.fold_in(key, 11)
    values, column_scale = rough_field(key, 0.3, 3.0)
    values = values * column_scale
    return jnp.clip(values, -200.0, 200.0).astype(jnp.bfloat16)


def block_scale(key, extent, cuts, low, top_value):
    def one(dim, blocks):
        draws = jax.random.uniform(jax.random.fold_in(jax.random.fold_in(key, 6), dim), (blocks,), jnp.float32, low / len(cuts), top_value / len(cuts))
        return jnp.repeat(jnp.exp(draws), extent[dim] // blocks).reshape((-1,) + (1,) * (len(extent) - dim - 1))

    level = one(*cuts[0])
    for cut in cuts[1:]:
        level = level * one(*cut)
    return level


def split_up(count, total, reach, slope):
    portions = [(1 << 20) // math.isqrt(standing ** slope) + 1 for standing in range(2, count + 1)]
    surplus, counts = total - reach - (count - 1), [1] * (count - 1)
    while surplus > 0:
        movable = [i for i in range(count - 1) if counts[i] < reach]
        whole, budget = sum([portions[i] for i in movable]), surplus
        for i in movable:
            addition = min(reach - counts[i], max(1, budget * portions[i] // whole), surplus)
            counts[i] = counts[i] + addition
            surplus = surplus - addition
    return np.array([reach] + counts)


def uneven(key, amount, total, bound, slope):
    if amount == 2:
        one = jax.random.randint(key, (), max(1, total - bound), min(bound, total - 1) + 1)
        return jnp.stack([one, total - one])
    lengths = jnp.asarray(split_up(amount, total, bound, slope), jnp.int32)
    couples = (amount - 1) // 2
    donor, taker = lengths[1:1 + 2 * couples:2], lengths[2:2 + 2 * couples:2]
    slack = jnp.minimum(donor - 1, bound - taker)
    passed = jax.random.randint(jax.random.fold_in(key, 1), (couples,), 0, 1 << 20) % (slack + 1)
    lengths = lengths.at[1:1 + 2 * couples:2].set(donor - passed).at[2:2 + 2 * couples:2].set(taker + passed)
    return lengths[jax.random.permutation(jax.random.fold_in(key, 2), amount)]


def centred(key, extent, spread, reach, cuts=(), held_as=jnp.bfloat16):
    values = spread * jax.random.normal(key, extent, jnp.float32)
    if cuts:
        values = values * block_scale(key, extent, cuts, -0.22, 0.18)
    return jnp.clip(values, -reach, reach).astype(held_as)


def setup_inputs(seed: int = 0) -> dict:
    streams_of = jax.random.split(jax.random.key(seed), 9)
    query_in = draw_query_in(jax.random.fold_in(streams_of[8], 71), 0)
    key_in = draw_key_in(jax.random.fold_in(streams_of[8], 71), 0)
    value_in = centred(streams_of[2], (TOKENS, WIDTH), 1.0, 6.0, ((0, 256),))
    out_cotangent = centred(streams_of[3], (TOKENS, WIDTH), 1.0, 6.0, ((0, 256),))
    query_gain = jnp.clip(jnp.exp(jax.random.uniform(streams_of[4], (WIDTH,), jnp.float32, math.log(0.8), math.log(2.5))), 0.8, 2.5)
    key_gain = jnp.clip(jnp.exp(jax.random.uniform(streams_of[5], (WIDTH,), jnp.float32, math.log(0.8), math.log(2.5))), 0.8, 2.5)
    frames = jax.vmap(lambda own: uneven(own, NVID, FRAMES_GRP, MOSTF, 2))(jax.random.split(streams_of[6], N_GRP)).reshape((N_GRP, NVID)).astype(jnp.int32)
    slab_group = jax.vmap(lambda own: jax.random.permutation(own, N_GRP))(jax.random.split(streams_of[7], N_GRP * N_SP)).reshape((N_GRP, N_SP, N_GRP)).astype(jnp.int32)
    return dict(query_in=query_in, key_in=key_in, value_in=value_in, out_cotangent=out_cotangent, query_gain=query_gain, key_gain=key_gain, frames=frames, slab_group=slab_group)


epsilon = 1e-06
masked_value = -1e+30

def normalize(values, gain):
    wide = values.astype(jnp.float32)
    factor = lax.rsqrt(lax.optimization_barrier(jnp.mean(wide * wide, axis=-1, keepdims=True)) + epsilon)
    return ((wide * factor * gain).astype(jnp.bfloat16), factor)

def normalize_back(values, gain, factor, upstream):
    wide = values.astype(jnp.float32)
    scaled = gain * upstream.astype(jnp.float32)
    inner = lax.optimization_barrier(jnp.mean(wide * scaled, axis=-1, keepdims=True))
    return (factor * scaled - wide * factor * factor * factor * inner).astype(jnp.bfloat16)

def slot_inverse(slab_group):
    slots = jnp.arange(N_GRP, dtype=jnp.int32)
    equal = slab_group[..., :, None] == slots
    return lax.optimization_barrier(jnp.sum(jnp.where(equal, slots[:, None], 0), axis=-2)).astype(jnp.int32)

def to_groups(values, inverse):
    split = values.reshape(N_GRP, N_SP, N_GRP, SLAB, WIDTH)
    picked = jnp.take_along_axis(split, inverse[:, :, :, None, None], axis=2)
    return picked.transpose(2, 1, 0, 3, 4).reshape(N_GRP, S_GRP, WIDTH)

def to_tokens(values, slab_group):
    split = values.reshape(N_GRP, N_SP, N_GRP, SLAB, WIDTH).transpose(2, 1, 0, 3, 4)
    picked = jnp.take_along_axis(split, slab_group[:, :, :, None, None], axis=2)
    return picked.reshape(TOKENS, WIDTH)

def split_heads(values):
    return values.reshape(S_GRP, HEADS, HDIM).transpose(1, 0, 2)

def join_heads(values):
    return values.transpose(1, 0, 2).reshape(S_GRP, WIDTH)

def group_pass(operands):
    query_group, key_group, value_group, cot_group, frame_counts = operands
    positions = jnp.arange(S_GRP, dtype=jnp.int32)
    video_ends = jnp.cumsum(frame_counts) * TOK_FRAME
    video_of = lax.optimization_barrier(jnp.sum((positions[:, None] >= video_ends[None, :]).astype(jnp.int32), axis=1))
    same_video = video_of[:, None] == video_of[None, :]
    scaling = 1.0 / math.sqrt(HDIM)

    def head_pass(head_operands):
        query_head, key_head, value_head, cot_head = head_operands
        scores = jnp.dot(query_head, key_head.T, preferred_element_type=jnp.float32) * scaling
        scores = jnp.where(same_video, scores, masked_value)
        row_max = lax.optimization_barrier(jnp.max(scores, axis=1, keepdims=True))
        log_total = row_max + jnp.log(lax.optimization_barrier(jnp.sum(jnp.exp(scores - row_max), axis=1, keepdims=True)))
        probs = jnp.exp(scores - log_total)
        weights = probs.astype(jnp.bfloat16)
        attended = jnp.dot(weights, value_head, preferred_element_type=jnp.float32).astype(jnp.bfloat16)
        row_dot = lax.optimization_barrier(jnp.sum(cot_head.astype(jnp.float32) * attended.astype(jnp.float32), axis=1, keepdims=True))
        dweights = jnp.dot(cot_head, value_head.T, preferred_element_type=jnp.float32)
        dscores = (probs * (dweights - row_dot)).astype(jnp.bfloat16)
        d_query = (jnp.dot(dscores, key_head, preferred_element_type=jnp.float32) * scaling).astype(jnp.bfloat16)
        d_key = (jnp.dot(dscores.T, query_head, preferred_element_type=jnp.float32) * scaling).astype(jnp.bfloat16)
        d_value = jnp.dot(weights.T, cot_head, preferred_element_type=jnp.float32).astype(jnp.bfloat16)
        return (attended, d_query, d_key, d_value)
    results = lax.map(head_pass, (split_heads(query_group), split_heads(key_group), split_heads(value_group), split_heads(cot_group)))
    return (join_heads(results[0]), join_heads(results[1]), join_heads(results[2]), join_heads(results[3]))

def reference(query_in, key_in, value_in, out_cotangent, query_gain, key_gain, frames, slab_group):
    query_norm, query_factor = normalize(query_in, query_gain)
    key_norm, key_factor = normalize(key_in, key_gain)
    inverse = slot_inverse(slab_group)
    grouped = lax.map(group_pass, (to_groups(query_norm, inverse), to_groups(key_norm, inverse), to_groups(value_in, inverse), to_groups(out_cotangent, inverse), frames))
    attn_out = to_tokens(grouped[0], slab_group)
    d_qnorm = to_tokens(grouped[1], slab_group)
    d_knorm = to_tokens(grouped[2], slab_group)
    grad_v = to_tokens(grouped[3], slab_group)
    grad_q = normalize_back(query_in, query_gain, query_factor, d_qnorm)
    grad_k = normalize_back(key_in, key_gain, key_factor, d_knorm)
    return (attn_out, grad_q, grad_k, grad_v)
```

```python
import math

import jax
import jax.numpy as jnp
from jax import lax
from jax.experimental import pallas as pl
from jax.experimental.pallas import tpu as pltpu
from jax.sharding import PartitionSpec as P

HDIM = 128
TOK_FRAME = 64
SLAB = 8
WIDTH = 4096
S_GRP = 2048
FRAMES_GRP = 32
NVID = 4
MOSTF = 21
N_GRP = 16
N_SP = 16
BIG = MOSTF * TOK_FRAME
REST = S_GRP - BIG
BIG_ROWS = 192
REST_ROWS = 176
PER_FRAME = TOK_FRAME // SLAB

EPSILON = 1e-06
MASKED = -1e30
SCALING = 1.0 / math.sqrt(HDIM)
LOG2E = math.log2(math.e)
MIB = 1 << 20

BF16 = jnp.bfloat16
F32 = jnp.float32


def rms_factor(wide):
    return lax.rsqrt(jnp.mean(wide * wide, axis=-1, keepdims=True) + EPSILON)


def pack_kernel(dest, q_ref, k_ref, v_ref, c_ref, qg_ref, kg_ref, first_ref, second_ref):
    def normalize(ref, gain_ref):
        wide = ref[0].astype(F32)
        return (wide * rms_factor(wide) * gain_ref[...]).astype(BF16)

    rows = (normalize(q_ref, qg_ref), normalize(k_ref, kg_ref), v_ref[0], c_ref[0])
    for owner in range(N_SP):
        for half, out_ref in enumerate((first_ref, second_ref)):
            start = (2 * owner + half) * HDIM
            for which in range(4):
                out_ref[0, owner, which] = rows[which][:, start : start + HDIM]


def pack(dest, query_in, key_in, value_in, cot, query_gain, key_gain):
    slab = pl.BlockSpec((1, SLAB, WIDTH), lambda j, d: (j, 0, 0))
    gain = pl.BlockSpec((1, WIDTH), lambda j, d: (0, 0))
    sent = pl.BlockSpec((1, N_SP, 4, SLAB, HDIM), lambda j, d: (d[j], 0, 0, 0, 0))
    shape = jax.ShapeDtypeStruct((N_GRP, N_SP, 4, SLAB, HDIM), BF16)
    return pl.pallas_call(
        pack_kernel,
        grid_spec=pltpu.PrefetchScalarGridSpec(
            num_scalar_prefetch=1,
            grid=(N_GRP,),
            in_specs=[slab, slab, slab, slab, gain, gain],
            out_specs=[sent, sent],
        ),
        out_shape=(shape, shape),
        compiler_params=pltpu.CompilerParams(vmem_limit_bytes=16 * MIB),
        name="pack",
    )(dest, query_in, key_in, value_in, cot, query_gain, key_gain)


def attend(q, c, keys, values, same):
    scores = lax.dot_general(q, keys, (((1,), (1,)), ((), ())), preferred_element_type=F32)
    if same is not None:
        scores = jnp.where(same, scores, MASKED)
    row_max = jnp.max(scores, axis=1, keepdims=True)
    grown = jnp.exp2((scores - row_max) * (SCALING * LOG2E))
    probs = grown * (1.0 / jnp.sum(grown, axis=1, keepdims=True))
    weights = probs.astype(BF16)
    attended = jnp.dot(weights, values, preferred_element_type=F32).astype(BF16)
    row_dot = jnp.sum(c.astype(F32) * attended.astype(F32), axis=1, keepdims=True)
    dweights = lax.dot_general(c, values, (((1,), (1,)), ((), ())), preferred_element_type=F32)
    dscores = (probs * (dweights - row_dot)).astype(BF16)
    d_query = jnp.dot(dscores, keys, preferred_element_type=F32) * SCALING
    over_rows = (((0,), (0,)), ((), ()))
    d_key = lax.dot_general(dscores, q, over_rows, preferred_element_type=F32)
    d_value = lax.dot_general(weights, c, over_rows, preferred_element_type=F32)
    return attended, d_query, d_key, d_value


def attention_kernel(frames, x_ref, out_ref, qs, ks, vs, cs, att, dqs, dks, dvs):
    counts = [frames[v] for v in range(NVID)]
    starts = [jnp.int32(0)]
    for v in range(NVID - 1):
        starts.append(starts[-1] + counts[v])
    before = jnp.int32(0)
    for v in range(NVID):
        before = before + jnp.where(counts[v] == MOSTF, starts[v], 0)

    def slot(frame):
        inside = jnp.logical_and(frame >= before, frame < before + MOSTF)
        outside = jnp.where(frame < before, frame + MOSTF, frame)
        return pl.multiple_of(jnp.where(inside, frame - before, outside) * TOK_FRAME, TOK_FRAME)

    for frame in range(FRAMES_GRP):
        rows = pl.ds(slot(frame), TOK_FRAME)
        part = slice((frame % 2) * PER_FRAME, (frame % 2 + 1) * PER_FRAME)
        for which, held in enumerate((qs, ks, vs, cs)):
            block = x_ref[part, frame // 2, which].astype(F32)
            held[rows, :] = block.reshape(TOK_FRAME, HDIM).astype(BF16)
    dks[...] = jnp.zeros_like(dks)
    dvs[...] = jnp.zeros_like(dvs)

    def section(first, length, block_rows, mask):
        def step(t, carry):
            rows = pl.ds(pl.multiple_of(first + t * block_rows, 16), block_rows)
            whole = pl.ds(first, length)
            attended, d_query, d_key, d_value = attend(
                qs[rows, :], cs[rows, :], ks[whole, :], vs[whole, :], mask(t)
            )
            att[rows, :] = attended
            dqs[rows, :] = d_query.astype(BF16)
            dks[whole, :] += d_key
            dvs[whole, :] += d_value
            return carry

        lax.fori_loop(0, length // block_rows, step, 0)

    def video_of(rest_index):
        position = rest_index + jnp.where(rest_index >= before * TOK_FRAME, BIG, 0)
        found = jnp.zeros_like(position)
        for v in range(1, NVID):
            found = found + (position >= starts[v] * TOK_FRAME).astype(jnp.int32)
        return found

    def rest_mask(t):
        down = lax.broadcasted_iota(jnp.int32, (REST_ROWS, 1), 0) + t * REST_ROWS
        across = lax.broadcasted_iota(jnp.int32, (1, REST), 1)
        return video_of(down) == video_of(across)

    section(0, BIG, BIG_ROWS, lambda t: None)
    section(BIG, REST, REST_ROWS, rest_mask)

    for frame in range(FRAMES_GRP):
        rows = pl.ds(slot(frame), TOK_FRAME)
        part = slice((frame % 2) * PER_FRAME, (frame % 2 + 1) * PER_FRAME)
        results = (
            att[rows, :].astype(F32),
            dqs[rows, :].astype(F32),
            dks[rows, :] * SCALING,
            dvs[rows, :],
        )
        for which in range(4):
            block = results[which].reshape(PER_FRAME, SLAB, HDIM)
            out_ref[part, frame // 2, which] = block.astype(BF16)


def attention(frames, received):
    held = pltpu.VMEM((S_GRP, HDIM), BF16)
    total = pltpu.VMEM((S_GRP, HDIM), F32)
    return pl.pallas_call(
        attention_kernel,
        in_specs=[
            pl.BlockSpec(memory_space=pltpu.SMEM),
            pl.BlockSpec(memory_space=pltpu.VMEM),
        ],
        out_specs=pl.BlockSpec(memory_space=pltpu.VMEM),
        out_shape=jax.ShapeDtypeStruct((N_GRP, N_SP, 4, SLAB, HDIM), BF16),
        scratch_shapes=[held, held, held, held, held, held, total, total],
        compiler_params=pltpu.CompilerParams(vmem_limit_bytes=40 * MIB),
        name="attention",
    )(frames, received)


def finish_kernel(
    dest, first_ref, second_ref, q_ref, k_ref, qg_ref, kg_ref, att_ref, gq_ref, gk_ref, gv_ref
):
    def joined(which):
        pieces = []
        for owner in range(N_SP):
            pieces.append(first_ref[0, owner, which])
            pieces.append(second_ref[0, owner, which])
        return jnp.concatenate(pieces, axis=1)

    def normalize_back(ref, gain_ref, upstream):
        wide = ref[0].astype(F32)
        factor = rms_factor(wide)
        scaled = gain_ref[...] * upstream.astype(F32)
        inner = jnp.mean(wide * scaled, axis=-1, keepdims=True)
        return (factor * scaled - wide * (factor * factor * factor * inner)).astype(BF16)

    att_ref[0] = joined(0)
    gq_ref[0] = normalize_back(q_ref, qg_ref, joined(1))
    gk_ref[0] = normalize_back(k_ref, kg_ref, joined(2))
    gv_ref[0] = joined(3)


def finish(dest, first, second, query_in, key_in, query_gain, key_gain):
    slab = pl.BlockSpec((1, SLAB, WIDTH), lambda j, d: (j, 0, 0))
    gain = pl.BlockSpec((1, WIDTH), lambda j, d: (0, 0))
    sent = pl.BlockSpec((1, N_SP, 4, SLAB, HDIM), lambda j, d: (d[j], 0, 0, 0, 0))
    shape = jax.ShapeDtypeStruct((N_GRP, SLAB, WIDTH), BF16)
    return pl.pallas_call(
        finish_kernel,
        grid_spec=pltpu.PrefetchScalarGridSpec(
            num_scalar_prefetch=1,
            grid=(N_GRP,),
            in_specs=[sent, sent, slab, slab, gain, gain],
            out_specs=[slab, slab, slab, slab],
        ),
        out_shape=(shape, shape, shape, shape),
        compiler_params=pltpu.CompilerParams(vmem_limit_bytes=16 * MIB),
        name="finish",
    )(dest, first, second, query_in, key_in, query_gain, key_gain)


def exchange(values):
    flat = values.reshape(N_GRP * N_SP, 4, SLAB, HDIM)
    moved = lax.all_to_all(flat, ("grp", "sp"), split_axis=0, concat_axis=0, tiled=True)
    return moved.reshape(N_GRP, N_SP, 4, SLAB, HDIM)


def local(query_in, key_in, value_in, out_cotangent, query_gain, key_gain, frames, slab_group):
    tokens, width = query_in.shape
    dest = slab_group.reshape(N_GRP)
    counts = frames.reshape(NVID)

    def slabs(values):
        return values.reshape(N_GRP, SLAB, width)

    gains = (query_gain.reshape(1, width), key_gain.reshape(1, width))
    sent = pack(
        dest, slabs(query_in), slabs(key_in), slabs(value_in), slabs(out_cotangent), *gains
    )
    received = [exchange(part) for part in sent]
    results = [attention(counts, part) for part in received]
    returned = [exchange(part) for part in results]
    outputs = finish(dest, returned[0], returned[1], slabs(query_in), slabs(key_in), *gains)
    return tuple(values.reshape(tokens, width) for values in outputs)


def solution(mesh):
    rows = P(("grp", "sp"), None)
    return jax.shard_map(
        local,
        mesh=mesh,
        in_specs=(rows, rows, rows, rows, P(), P(), P("grp", None), P("grp", "sp", None)),
        out_specs=(rows, rows, rows, rows),
        check_vma=False,
    )
```

```python
import math

import jax
import jax.numpy as jnp
from jax import lax
from jax.experimental import pallas as pl
from jax.experimental.pallas import tpu as pltpu
from jax.sharding import PartitionSpec as P

HDIM = 128
TOK_FRAME = 64
SLAB = 8
WIDTH = 4096
S_GRP = 2048
FRAMES_GRP = 32
NVID = 4
MOSTF = 21
N_GRP = 16
N_SP = 16
BIG = MOSTF * TOK_FRAME
REST = S_GRP - BIG
PER_FRAME = TOK_FRAME // SLAB
PAIR = 2 * HDIM
PART = 4

EPSILON = 1e-06
MASKED = -1e30
SCALING = 1.0 / math.sqrt(HDIM)
LOG2E = math.log2(math.e)
MIB = 1 << 20
ATT_VMEM = 40 * MIB

BF16 = jnp.bfloat16
F32 = jnp.float32


def rms_factor(wide):
    return lax.rsqrt(jnp.mean(wide * wide, axis=-1, keepdims=True) + EPSILON)


def pack_kernel(dest, q_ref, k_ref, v_ref, c_ref, qg_ref, kg_ref, out_ref, held, arrived):
    def fetch(which, part):
        source = (q_ref, k_ref, v_ref, c_ref)[which]
        rows = pl.ds(part * PART, PART)
        return pltpu.make_async_copy(
            source.at[rows], held.at[which, rows], arrived.at[which, part]
        )

    for part in range(N_GRP // PART):
        for which in range(4):
            fetch(which, part).start()

    def normalize(values, gain_ref):
        wide = values.astype(F32)
        return (wide * rms_factor(wide) * gain_ref[...]).astype(BF16)

    for part in range(N_GRP // PART):
        for which in range(4):
            fetch(which, part).wait()
        for slab in range(part * PART, (part + 1) * PART):
            rows = (
                normalize(held[0, slab], qg_ref),
                normalize(held[1, slab], kg_ref),
                held[2, slab],
                held[3, slab],
            )
            for owner in range(N_SP):
                for which in range(4):
                    piece = rows[which][:, owner * PAIR : (owner + 1) * PAIR]
                    out_ref[dest[slab], owner, which] = piece


def pack(dest, query_in, key_in, value_in, cot, query_gain, key_gain):
    smem = pl.BlockSpec(memory_space=pltpu.SMEM)
    vmem = pl.BlockSpec(memory_space=pltpu.VMEM)
    hbm = pl.BlockSpec(memory_space=pl.ANY)
    return pl.pallas_call(
        pack_kernel,
        in_specs=[smem, hbm, hbm, hbm, hbm, vmem, vmem],
        out_specs=vmem,
        out_shape=jax.ShapeDtypeStruct((N_GRP, N_SP, 4, SLAB, PAIR), BF16),
        scratch_shapes=[
            pltpu.VMEM((4, N_GRP, SLAB, WIDTH), BF16),
            pltpu.SemaphoreType.DMA((4, N_GRP // PART)),
        ],
        compiler_params=pltpu.CompilerParams(vmem_limit_bytes=32 * MIB),
        name="pack",
    )(dest, query_in, key_in, value_in, cot, query_gain, key_gain)


def attend(q, keys, values, c, same):
    rows = (((1,), (1,)), ((), ()))
    over_rows = (((0,), (0,)), ((), ()))
    scores = lax.dot_general(q, keys, rows, preferred_element_type=F32)
    if same is not None:
        scores = jnp.where(same, scores, MASKED)
    row_max = jnp.max(scores, axis=1, keepdims=True)
    grown = jnp.exp2((scores - row_max) * (SCALING * LOG2E))
    probs = grown * (1.0 / jnp.sum(grown, axis=1, keepdims=True))
    weights = probs.astype(BF16)
    attended = jnp.dot(weights, values, preferred_element_type=F32).astype(BF16)
    row_dot = jnp.sum(c.astype(F32) * attended.astype(F32), axis=1, keepdims=True)
    dweights = lax.dot_general(c, values, rows, preferred_element_type=F32)
    dscores = (probs * (dweights - row_dot)).astype(BF16)
    d_query = jnp.dot(dscores, keys, preferred_element_type=F32) * SCALING
    d_key = lax.dot_general(dscores, q, over_rows, preferred_element_type=F32) * SCALING
    d_value = lax.dot_general(weights, c, over_rows, preferred_element_type=F32)
    return attended, d_query, d_key, d_value


def attention_kernel(frames, x_ref, out_ref, *held):
    counts = [frames[v] for v in range(NVID)]
    starts = [jnp.int32(0)]
    for v in range(NVID - 1):
        starts.append(starts[-1] + counts[v])
    before = jnp.int32(0)
    for v in range(NVID):
        before = before + jnp.where(counts[v] == MOSTF, starts[v], 0)

    def frame_rows(frame):
        inside = jnp.logical_and(frame >= before, frame < before + MOSTF)
        outside = jnp.where(frame < before, frame + MOSTF, frame)
        slot = jnp.where(inside, frame - before, outside) * TOK_FRAME
        return pl.ds(pl.multiple_of(slot, TOK_FRAME), TOK_FRAME)

    def video_of(rest_index):
        position = rest_index + jnp.where(rest_index >= before * TOK_FRAME, BIG, 0)
        found = jnp.zeros_like(position)
        for v in range(1, NVID):
            found = found + (position >= starts[v] * TOK_FRAME).astype(jnp.int32)
        return found

    down = lax.broadcasted_iota(jnp.int32, (REST, 1), 0)
    across = lax.broadcasted_iota(jnp.int32, (1, REST), 1)
    same = video_of(down) == video_of(across)
    slots = [frame_rows(frame) for frame in range(FRAMES_GRP)]

    def slab_rows(frame):
        return slice((frame % 2) * PER_FRAME, (frame % 2 + 1) * PER_FRAME)

    for head in range(2):
        lanes = slice(head * HDIM, (head + 1) * HDIM)
        ins, outs = held[8 * head : 8 * head + 4], held[8 * head + 4 : 8 * head + 8]
        for frame in range(FRAMES_GRP):
            for which in range(4):
                block = x_ref[slab_rows(frame), frame // 2, which, :, lanes].astype(F32)
                ins[which][slots[frame], :] = block.reshape(TOK_FRAME, HDIM).astype(BF16)
        for section, mask in ((slice(0, BIG), None), (slice(BIG, S_GRP), same)):
            results = attend(*(ref[section, :] for ref in ins), mask)
            for which in range(4):
                outs[which][section, :] = results[which].astype(outs[which].dtype)
        for frame in range(FRAMES_GRP):
            for which in range(4):
                block = outs[which][slots[frame], :].astype(F32).reshape(PER_FRAME, SLAB, HDIM)
                out_ref[slab_rows(frame), frame // 2, which, :, lanes] = block.astype(BF16)


def attention(frames, received):
    held = [pltpu.VMEM((S_GRP, HDIM), BF16)] * 16
    return pl.pallas_call(
        attention_kernel,
        in_specs=[
            pl.BlockSpec(memory_space=pltpu.SMEM),
            pl.BlockSpec(memory_space=pltpu.VMEM),
        ],
        out_specs=pl.BlockSpec(memory_space=pltpu.VMEM),
        out_shape=jax.ShapeDtypeStruct((N_GRP, N_SP, 4, SLAB, PAIR), BF16),
        scratch_shapes=held,
        compiler_params=pltpu.CompilerParams(vmem_limit_bytes=ATT_VMEM),
        name="attention",
    )(frames, received)


def finish_kernel(
    dest, x_ref, q_ref, k_ref, qg_ref, kg_ref, att_ref, gq_ref, gk_ref, gv_ref, held, gone
):
    def store(which, part):
        target = (att_ref, gq_ref, gk_ref, gv_ref)[which]
        rows = pl.ds(part * PART, PART)
        return pltpu.make_async_copy(held.at[which, rows], target.at[rows], gone.at[which, part])

    def normalize_back(values, gain_ref, upstream):
        wide = values.astype(F32)
        factor = rms_factor(wide)
        scaled = gain_ref[...] * upstream.astype(F32)
        inner = jnp.mean(wide * scaled, axis=-1, keepdims=True)
        return (factor * scaled - wide * (factor * factor * factor * inner)).astype(BF16)

    for part in range(N_GRP // PART):
        for which in (0, 3):
            for slab in range(part * PART, (part + 1) * PART):
                for owner in range(N_SP):
                    columns = slice(owner * PAIR, (owner + 1) * PAIR)
                    held[which, slab, :, columns] = x_ref[dest[slab], owner, which]
            store(which, part).start()
    for part in range(N_GRP // PART):
        for which, source, gain_ref in ((1, q_ref, qg_ref), (2, k_ref, kg_ref)):
            for slab in range(part * PART, (part + 1) * PART):
                pieces = [x_ref[dest[slab], owner, which] for owner in range(N_SP)]
                upstream = jnp.concatenate(pieces, axis=1)
                held[which, slab] = normalize_back(source[slab], gain_ref, upstream)
            store(which, part).start()
    for part in range(N_GRP // PART):
        for which in range(4):
            store(which, part).wait()


def finish(dest, returned, query_in, key_in, query_gain, key_gain):
    smem = pl.BlockSpec(memory_space=pltpu.SMEM)
    vmem = pl.BlockSpec(memory_space=pltpu.VMEM)
    hbm = pl.BlockSpec(memory_space=pl.ANY)
    return pl.pallas_call(
        finish_kernel,
        in_specs=[smem, vmem, vmem, vmem, vmem, vmem],
        out_specs=[hbm, hbm, hbm, hbm],
        out_shape=[jax.ShapeDtypeStruct((N_GRP, SLAB, WIDTH), BF16)] * 4,
        scratch_shapes=[
            pltpu.VMEM((4, N_GRP, SLAB, WIDTH), BF16),
            pltpu.SemaphoreType.DMA((4, N_GRP // PART)),
        ],
        compiler_params=pltpu.CompilerParams(vmem_limit_bytes=32 * MIB),
        name="finish",
    )(dest, returned, query_in, key_in, query_gain, key_gain)


def exchange(values):
    flat = values.reshape(N_GRP * N_SP, 4, SLAB, PAIR)
    moved = lax.all_to_all(flat, ("grp", "sp"), split_axis=0, concat_axis=0, tiled=True)
    return moved.reshape(values.shape)


def local(query_in, key_in, value_in, out_cotangent, query_gain, key_gain, frames, slab_group):
    tokens, width = query_in.shape
    dest = slab_group.reshape(N_GRP)

    def slabs(values):
        return values.reshape(N_GRP, SLAB, width)

    gains = (query_gain.reshape(1, width), key_gain.reshape(1, width))
    sent = pack(
        dest, slabs(query_in), slabs(key_in), slabs(value_in), slabs(out_cotangent), *gains
    )
    results = attention(frames.reshape(NVID), exchange(sent))
    outputs = finish(dest, exchange(results), slabs(query_in), slabs(key_in), *gains)
    return tuple(values.reshape(tokens, width) for values in outputs)


def solution(mesh):
    rows = P(("grp", "sp"), None)
    return jax.shard_map(
        local,
        mesh=mesh,
        in_specs=(rows, rows, rows, rows, P(), P(), P("grp", None), P("grp", "sp", None)),
        out_specs=(rows, rows, rows, rows),
        check_vma=False,
    )
```

```python
import math

import jax
import jax.numpy as jnp
from jax import lax
from jax.experimental import pallas as pl
from jax.experimental.pallas import tpu as pltpu
from jax.sharding import PartitionSpec as P

HDIM = 128
TOK_FRAME = 64
SLAB = 8
WIDTH = 4096
S_GRP = 2048
FRAMES_GRP = 32
NVID = 4
MOSTF = 21
N_GRP = 16
N_SP = 16
BIG = MOSTF * TOK_FRAME
REST = S_GRP - BIG
PER_FRAME = TOK_FRAME // SLAB
PAIR = 2 * HDIM
PART = 4

EPSILON = 1e-06
MASKED = -1e30
SCALING = 1.0 / math.sqrt(HDIM)
LOG2E = math.log2(math.e)
MIB = 1 << 20
ATT_VMEM = 40 * MIB

BF16 = jnp.bfloat16
F32 = jnp.float32


def rms_factor(wide):
    return lax.rsqrt(jnp.mean(wide * wide, axis=-1, keepdims=True) + EPSILON)


def pack_kernel(
    dest, q_ref, k_ref, v_ref, c_ref, qg_hbm, kg_hbm, out_ref, held, qg_ref, kg_ref, arrived, ready
):
    gains = (
        pltpu.make_async_copy(qg_hbm, qg_ref, ready.at[0]),
        pltpu.make_async_copy(kg_hbm, kg_ref, ready.at[1]),
    )
    def fetch(which, part):
        source = (q_ref, k_ref, v_ref, c_ref)[which]
        rows = pl.ds(part * PART, PART)
        return pltpu.make_async_copy(
            source.at[rows], held.at[which, rows], arrived.at[which, part]
        )

    for copy in gains:
        copy.start()
    for part in range(N_GRP // PART):
        for which in range(4):
            fetch(which, part).start()
    for copy in gains:
        copy.wait()

    def normalize(values, gain_ref):
        wide = values.astype(F32)
        return (wide * rms_factor(wide) * gain_ref[...]).astype(BF16)

    for part in range(N_GRP // PART):
        for which in range(4):
            fetch(which, part).wait()
        for slab in range(part * PART, (part + 1) * PART):
            rows = (
                normalize(held[0, slab], qg_ref),
                normalize(held[1, slab], kg_ref),
                held[2, slab],
                held[3, slab],
            )
            for owner in range(N_SP):
                for which in range(4):
                    piece = rows[which][:, owner * PAIR : (owner + 1) * PAIR]
                    out_ref[dest[slab], owner, which] = piece


def pack(dest, query_in, key_in, value_in, cot, query_gain, key_gain):
    smem = pl.BlockSpec(memory_space=pltpu.SMEM)
    vmem = pl.BlockSpec(memory_space=pltpu.VMEM)
    hbm = pl.BlockSpec(memory_space=pltpu.HBM)
    operands = [
        pltpu.with_memory_space_constraint(values, pltpu.HBM)
        for values in (dest, query_in, key_in, value_in, cot, query_gain, key_gain)
    ]
    return pl.pallas_call(
        pack_kernel,
        in_specs=[smem, hbm, hbm, hbm, hbm, hbm, hbm],
        out_specs=vmem,
        out_shape=jax.ShapeDtypeStruct((N_GRP, N_SP, 4, SLAB, PAIR), BF16),
        scratch_shapes=[
            pltpu.VMEM((4, N_GRP, SLAB, WIDTH), BF16),
            pltpu.VMEM((1, WIDTH), F32),
            pltpu.VMEM((1, WIDTH), F32),
            pltpu.SemaphoreType.DMA((4, N_GRP // PART)),
            pltpu.SemaphoreType.DMA((2,)),
        ],
        compiler_params=pltpu.CompilerParams(vmem_limit_bytes=32 * MIB),
        name="pack",
    )(*operands)


def attend(q, keys, values, c, same):
    rows = (((1,), (1,)), ((), ()))
    over_rows = (((0,), (0,)), ((), ()))
    scores = lax.dot_general(q, keys, rows, preferred_element_type=F32)
    if same is not None:
        scores = jnp.where(same, scores, MASKED)
    row_max = jnp.max(scores, axis=1, keepdims=True)
    grown = jnp.exp2((scores - row_max) * (SCALING * LOG2E))
    probs = grown * (1.0 / jnp.sum(grown, axis=1, keepdims=True))
    weights = probs.astype(BF16)
    attended = jnp.dot(weights, values, preferred_element_type=F32).astype(BF16)
    row_dot = jnp.sum(c.astype(F32) * attended.astype(F32), axis=1, keepdims=True)
    dweights = lax.dot_general(c, values, rows, preferred_element_type=F32)
    dscores = (probs * (dweights - row_dot)).astype(BF16)
    d_query = jnp.dot(dscores, keys, preferred_element_type=F32) * SCALING
    d_key = lax.dot_general(dscores, q, over_rows, preferred_element_type=F32) * SCALING
    d_value = lax.dot_general(weights, c, over_rows, preferred_element_type=F32)
    return attended, d_query, d_key, d_value


def attention_kernel(frames, x_ref, out_ref, *held):
    counts = [frames[v] for v in range(NVID)]
    starts = [jnp.int32(0)]
    for v in range(NVID - 1):
        starts.append(starts[-1] + counts[v])
    before = jnp.int32(0)
    for v in range(NVID):
        before = before + jnp.where(counts[v] == MOSTF, starts[v], 0)

    def frame_rows(frame):
        inside = jnp.logical_and(frame >= before, frame < before + MOSTF)
        outside = jnp.where(frame < before, frame + MOSTF, frame)
        slot = jnp.where(inside, frame - before, outside) * TOK_FRAME
        return pl.ds(pl.multiple_of(slot, TOK_FRAME), TOK_FRAME)

    def video_of(rest_index):
        position = rest_index + jnp.where(rest_index >= before * TOK_FRAME, BIG, 0)
        found = jnp.zeros_like(position)
        for v in range(1, NVID):
            found = found + (position >= starts[v] * TOK_FRAME).astype(jnp.int32)
        return found

    down = lax.broadcasted_iota(jnp.int32, (REST, 1), 0)
    across = lax.broadcasted_iota(jnp.int32, (1, REST), 1)
    same = video_of(down) == video_of(across)
    slots = [frame_rows(frame) for frame in range(FRAMES_GRP)]

    def slab_rows(frame):
        return slice((frame % 2) * PER_FRAME, (frame % 2 + 1) * PER_FRAME)

    for head in range(2):
        lanes = slice(head * HDIM, (head + 1) * HDIM)
        ins, outs = held[8 * head : 8 * head + 4], held[8 * head + 4 : 8 * head + 8]
        for frame in range(FRAMES_GRP):
            for which in range(4):
                block = x_ref[slab_rows(frame), frame // 2, which, :, lanes].astype(F32)
                ins[which][slots[frame], :] = block.reshape(TOK_FRAME, HDIM).astype(BF16)
        for section, mask in ((slice(0, BIG), None), (slice(BIG, S_GRP), same)):
            results = attend(*(ref[section, :] for ref in ins), mask)
            for which in range(4):
                outs[which][section, :] = results[which].astype(outs[which].dtype)
        for frame in range(FRAMES_GRP):
            for which in range(4):
                block = outs[which][slots[frame], :].astype(F32).reshape(PER_FRAME, SLAB, HDIM)
                out_ref[slab_rows(frame), frame // 2, which, :, lanes] = block.astype(BF16)


def attention(frames, received):
    held = [pltpu.VMEM((S_GRP, HDIM), BF16)] * 16
    return pl.pallas_call(
        attention_kernel,
        in_specs=[
            pl.BlockSpec(memory_space=pltpu.SMEM),
            pl.BlockSpec(memory_space=pltpu.VMEM),
        ],
        out_specs=pl.BlockSpec(memory_space=pltpu.VMEM),
        out_shape=jax.ShapeDtypeStruct((N_GRP, N_SP, 4, SLAB, PAIR), BF16),
        scratch_shapes=held,
        compiler_params=pltpu.CompilerParams(vmem_limit_bytes=ATT_VMEM),
        name="attention",
    )(frames, received)


def finish_kernel(
    dest, x_ref, q_ref, k_ref, qg_ref, kg_ref, att_ref, gq_ref, gk_ref, gv_ref, held, gone
):
    def store(which, part):
        target = (att_ref, gq_ref, gk_ref, gv_ref)[which]
        rows = pl.ds(part * PART, PART)
        return pltpu.make_async_copy(held.at[which, rows], target.at[rows], gone.at[which, part])

    def normalize_back(values, gain_ref, upstream):
        wide = values.astype(F32)
        factor = rms_factor(wide)
        scaled = gain_ref[...] * upstream.astype(F32)
        inner = jnp.mean(wide * scaled, axis=-1, keepdims=True)
        return (factor * scaled - wide * (factor * factor * factor * inner)).astype(BF16)

    for part in range(N_GRP // PART):
        for which in (0, 3):
            for slab in range(part * PART, (part + 1) * PART):
                for owner in range(N_SP):
                    columns = slice(owner * PAIR, (owner + 1) * PAIR)
                    held[which, slab, :, columns] = x_ref[dest[slab], owner, which]
            store(which, part).start()
    for part in range(N_GRP // PART):
        for which, source, gain_ref in ((1, q_ref, qg_ref), (2, k_ref, kg_ref)):
            for slab in range(part * PART, (part + 1) * PART):
                pieces = [x_ref[dest[slab], owner, which] for owner in range(N_SP)]
                upstream = jnp.concatenate(pieces, axis=1)
                held[which, slab] = normalize_back(source[slab], gain_ref, upstream)
            store(which, part).start()
    for part in range(N_GRP // PART):
        for which in range(4):
            store(which, part).wait()


def finish(dest, returned, query_in, key_in, query_gain, key_gain):
    smem = pl.BlockSpec(memory_space=pltpu.SMEM)
    vmem = pl.BlockSpec(memory_space=pltpu.VMEM)
    hbm = pl.BlockSpec(memory_space=pl.ANY)
    return pl.pallas_call(
        finish_kernel,
        in_specs=[smem, vmem, vmem, vmem, vmem, vmem],
        out_specs=[hbm, hbm, hbm, hbm],
        out_shape=[jax.ShapeDtypeStruct((N_GRP, SLAB, WIDTH), BF16)] * 4,
        scratch_shapes=[
            pltpu.VMEM((4, N_GRP, SLAB, WIDTH), BF16),
            pltpu.SemaphoreType.DMA((4, N_GRP // PART)),
        ],
        compiler_params=pltpu.CompilerParams(vmem_limit_bytes=32 * MIB),
        name="finish",
    )(dest, returned, query_in, key_in, query_gain, key_gain)


def exchange(values):
    flat = values.reshape(N_GRP * N_SP, 4, SLAB, PAIR)
    moved = lax.all_to_all(flat, ("grp", "sp"), split_axis=0, concat_axis=0, tiled=True)
    return moved.reshape(values.shape)


def local(query_in, key_in, value_in, out_cotangent, query_gain, key_gain, frames, slab_group):
    tokens, width = query_in.shape
    dest = slab_group.reshape(N_GRP)

    def slabs(values):
        return values.reshape(N_GRP, SLAB, width)

    gains = (query_gain.reshape(1, width), key_gain.reshape(1, width))
    sent = pack(
        dest, slabs(query_in), slabs(key_in), slabs(value_in), slabs(out_cotangent), *gains
    )
    results = attention(frames.reshape(NVID), exchange(sent))
    outputs = finish(dest, exchange(results), slabs(query_in), slabs(key_in), *gains)
    return tuple(values.reshape(tokens, width) for values in outputs)


def solution(mesh):
    rows = P(("grp", "sp"), None)
    return jax.shard_map(
        local,
        mesh=mesh,
        in_specs=(rows, rows, rows, rows, P(), P(), P("grp", None), P("grp", "sp", None)),
        out_specs=(rows, rows, rows, rows),
        check_vma=False,
    )
```

```python
import math

import jax
import jax.numpy as jnp
from jax import lax
from jax.experimental import pallas as pl
from jax.experimental.pallas import tpu as pltpu
from jax.sharding import PartitionSpec as P

HDIM = 128
TOK_FRAME = 64
SLAB = 8
WIDTH = 4096
S_GRP = 2048
FRAMES_GRP = 32
NVID = 4
MOSTF = 21
N_GRP = 16
N_SP = 16
BIG = MOSTF * TOK_FRAME
REST = S_GRP - BIG
PER_FRAME = TOK_FRAME // SLAB
PAIR = 2 * HDIM
PART = 4

EPSILON = 1e-06
MASKED = -1e30
SCALING = 1.0 / math.sqrt(HDIM)
LOG2E = math.log2(math.e)
MIB = 1 << 20
ATT_VMEM = 40 * MIB

BF16 = jnp.bfloat16
F32 = jnp.float32


def rms_factor(wide):
    return lax.rsqrt(jnp.mean(wide * wide, axis=-1, keepdims=True) + EPSILON)


def pack_kernel(
    dest, q_ref, k_ref, v_ref, c_ref, qg_hbm, kg_hbm, out_ref, held, qg_ref, kg_ref, arrived, ready
):
    gains = (
        pltpu.make_async_copy(qg_hbm, qg_ref, ready.at[0]),
        pltpu.make_async_copy(kg_hbm, kg_ref, ready.at[1]),
    )
    def fetch(which, part):
        source = (q_ref, k_ref, v_ref, c_ref)[which]
        rows = pl.ds(part * PART, PART)
        return pltpu.make_async_copy(
            source.at[rows], held.at[which, rows], arrived.at[which, part]
        )

    for copy in gains:
        copy.start()
    for part in range(N_GRP // PART):
        for which in range(4):
            fetch(which, part).start()
    for copy in gains:
        copy.wait()

    def normalize(values, gain_ref):
        wide = values.astype(F32)
        return (wide * rms_factor(wide) * gain_ref[...]).astype(BF16)

    for part in range(N_GRP // PART):
        for which in range(4):
            fetch(which, part).wait()
        for slab in range(part * PART, (part + 1) * PART):
            rows = (
                normalize(held[0, slab], qg_ref),
                normalize(held[1, slab], kg_ref),
                held[2, slab],
                held[3, slab],
            )
            for owner in range(N_SP):
                for which in range(4):
                    piece = rows[which][:, owner * PAIR : (owner + 1) * PAIR]
                    out_ref[dest[slab], owner, which] = piece


def pack(dest, query_in, key_in, value_in, cot, query_gain, key_gain):
    smem = pl.BlockSpec(memory_space=pltpu.SMEM)
    vmem = pl.BlockSpec(memory_space=pltpu.VMEM)
    hbm = pl.BlockSpec(memory_space=pltpu.HBM)
    operands = [
        pltpu.with_memory_space_constraint(values, pltpu.HBM)
        for values in (dest, query_in, key_in, value_in, cot, query_gain, key_gain)
    ]
    return pl.pallas_call(
        pack_kernel,
        in_specs=[smem, hbm, hbm, hbm, hbm, hbm, hbm],
        out_specs=vmem,
        out_shape=jax.ShapeDtypeStruct((N_GRP, N_SP, 4, SLAB, PAIR), BF16),
        scratch_shapes=[
            pltpu.VMEM((4, N_GRP, SLAB, WIDTH), BF16),
            pltpu.VMEM((1, WIDTH), F32),
            pltpu.VMEM((1, WIDTH), F32),
            pltpu.SemaphoreType.DMA((4, N_GRP // PART)),
            pltpu.SemaphoreType.DMA((2,)),
        ],
        compiler_params=pltpu.CompilerParams(vmem_limit_bytes=32 * MIB),
        name="pack",
    )(*operands)


def attend(q, keys, values, c, same):
    rows = (((1,), (1,)), ((), ()))
    over_rows = (((0,), (0,)), ((), ()))
    scores = lax.dot_general(q, keys, rows, preferred_element_type=F32)
    if same is not None:
        scores = jnp.where(same, scores, MASKED)
    row_max = jnp.max(scores, axis=1, keepdims=True)
    grown = jnp.exp2((scores - row_max) * (SCALING * LOG2E))
    probs = grown * (1.0 / jnp.sum(grown, axis=1, keepdims=True))
    weights = probs.astype(BF16)
    attended = jnp.dot(weights, values, preferred_element_type=F32).astype(BF16)
    row_dot = jnp.sum(c.astype(F32) * attended.astype(F32), axis=1, keepdims=True)
    dweights = lax.dot_general(c, values, rows, preferred_element_type=F32)
    dscores = (probs * (dweights - row_dot)).astype(BF16)
    d_query = jnp.dot(dscores, keys, preferred_element_type=F32) * SCALING
    d_key = lax.dot_general(q, dscores, over_rows, preferred_element_type=F32) * SCALING
    d_value = lax.dot_general(c, weights, over_rows, preferred_element_type=F32)
    return attended, d_query, d_key.T, d_value.T


def attention_kernel(frames, x_ref, out_ref, *held):
    counts = [frames[v] for v in range(NVID)]
    starts = [jnp.int32(0)]
    for v in range(NVID - 1):
        starts.append(starts[-1] + counts[v])
    before = jnp.int32(0)
    for v in range(NVID):
        before = before + jnp.where(counts[v] == MOSTF, starts[v], 0)

    def frame_rows(frame):
        inside = jnp.logical_and(frame >= before, frame < before + MOSTF)
        outside = jnp.where(frame < before, frame + MOSTF, frame)
        slot = jnp.where(inside, frame - before, outside) * TOK_FRAME
        return pl.ds(pl.multiple_of(slot, TOK_FRAME), TOK_FRAME)

    def video_of(rest_index):
        position = rest_index + jnp.where(rest_index >= before * TOK_FRAME, BIG, 0)
        found = jnp.zeros_like(position)
        for v in range(1, NVID):
            found = found + (position >= starts[v] * TOK_FRAME).astype(jnp.int32)
        return found

    down = lax.broadcasted_iota(jnp.int32, (REST, 1), 0)
    across = lax.broadcasted_iota(jnp.int32, (1, REST), 1)
    same = video_of(down) == video_of(across)
    slots = [frame_rows(frame) for frame in range(FRAMES_GRP)]

    def slab_rows(frame):
        return slice((frame % 2) * PER_FRAME, (frame % 2 + 1) * PER_FRAME)

    for frame in range(FRAMES_GRP):
        for which in range(4):
            block = x_ref[slab_rows(frame), frame // 2, which].astype(F32)
            block = block.reshape(TOK_FRAME, PAIR).astype(BF16)
            for head in range(2):
                lanes = slice(head * HDIM, (head + 1) * HDIM)
                held[8 * head + which][slots[frame], :] = block[:, lanes]
    for head in range(2):
        ins, outs = held[8 * head : 8 * head + 4], held[8 * head + 4 : 8 * head + 8]
        for section, mask in ((slice(0, BIG), None), (slice(BIG, S_GRP), same)):
            results = attend(*(ref[section, :] for ref in ins), mask)
            for which in range(4):
                outs[which][section, :] = results[which].astype(BF16)
    for frame in range(FRAMES_GRP):
        for which in range(4):
            pair = [held[8 * head + 4 + which][slots[frame], :] for head in range(2)]
            block = jnp.concatenate(pair, axis=1).astype(F32)
            block = block.reshape(PER_FRAME, SLAB, PAIR)
            out_ref[slab_rows(frame), frame // 2, which] = block.astype(BF16)


def attention(frames, received):
    held = [pltpu.VMEM((S_GRP, HDIM), BF16)] * 16
    return pl.pallas_call(
        attention_kernel,
        in_specs=[
            pl.BlockSpec(memory_space=pltpu.SMEM),
            pl.BlockSpec(memory_space=pltpu.VMEM),
        ],
        out_specs=pl.BlockSpec(memory_space=pltpu.VMEM),
        out_shape=jax.ShapeDtypeStruct((N_GRP, N_SP, 4, SLAB, PAIR), BF16),
        scratch_shapes=held,
        compiler_params=pltpu.CompilerParams(vmem_limit_bytes=ATT_VMEM),
        name="attention",
    )(frames, received)


def finish_kernel(
    dest, x_ref, q_ref, k_ref, qg_ref, kg_ref, att_ref, gq_ref, gk_ref, gv_ref, held, gone
):
    def store(which, part):
        target = (att_ref, gq_ref, gk_ref, gv_ref)[which]
        rows = pl.ds(part * PART, PART)
        return pltpu.make_async_copy(held.at[which, rows], target.at[rows], gone.at[which, part])

    def normalize_back(values, gain_ref, upstream):
        wide = values.astype(F32)
        factor = rms_factor(wide)
        scaled = gain_ref[...] * upstream.astype(F32)
        inner = jnp.mean(wide * scaled, axis=-1, keepdims=True)
        return (factor * scaled - wide * (factor * factor * factor * inner)).astype(BF16)

    for part in range(N_GRP // PART):
        for which in (0, 3):
            for slab in range(part * PART, (part + 1) * PART):
                for owner in range(N_SP):
                    columns = slice(owner * PAIR, (owner + 1) * PAIR)
                    held[which, slab, :, columns] = x_ref[dest[slab], owner, which]
            store(which, part).start()
    for part in range(N_GRP // PART):
        for which, source, gain_ref in ((1, q_ref, qg_ref), (2, k_ref, kg_ref)):
            for slab in range(part * PART, (part + 1) * PART):
                pieces = [x_ref[dest[slab], owner, which] for owner in range(N_SP)]
                upstream = jnp.concatenate(pieces, axis=1)
                held[which, slab] = normalize_back(source[slab], gain_ref, upstream)
            store(which, part).start()
    for part in range(N_GRP // PART):
        for which in range(4):
            store(which, part).wait()


def finish(dest, returned, query_in, key_in, query_gain, key_gain):
    smem = pl.BlockSpec(memory_space=pltpu.SMEM)
    vmem = pl.BlockSpec(memory_space=pltpu.VMEM)
    hbm = pl.BlockSpec(memory_space=pl.ANY)
    return pl.pallas_call(
        finish_kernel,
        in_specs=[smem, vmem, vmem, vmem, vmem, vmem],
        out_specs=[hbm, hbm, hbm, hbm],
        out_shape=[jax.ShapeDtypeStruct((N_GRP, SLAB, WIDTH), BF16)] * 4,
        scratch_shapes=[
            pltpu.VMEM((4, N_GRP, SLAB, WIDTH), BF16),
            pltpu.SemaphoreType.DMA((4, N_GRP // PART)),
        ],
        compiler_params=pltpu.CompilerParams(vmem_limit_bytes=32 * MIB),
        name="finish",
    )(dest, returned, query_in, key_in, query_gain, key_gain)


def exchange(values):
    flat = values.reshape(N_GRP * N_SP, 4, SLAB, PAIR)
    moved = lax.all_to_all(flat, ("grp", "sp"), split_axis=0, concat_axis=0, tiled=True)
    return moved.reshape(values.shape)


def local(query_in, key_in, value_in, out_cotangent, query_gain, key_gain, frames, slab_group):
    tokens, width = query_in.shape
    dest = slab_group.reshape(N_GRP)

    def slabs(values):
        return values.reshape(N_GRP, SLAB, width)

    gains = (query_gain.reshape(1, width), key_gain.reshape(1, width))
    sent = pack(
        dest, slabs(query_in), slabs(key_in), slabs(value_in), slabs(out_cotangent), *gains
    )
    results = attention(frames.reshape(NVID), exchange(sent))
    outputs = finish(dest, exchange(results), slabs(query_in), slabs(key_in), *gains)
    return tuple(values.reshape(tokens, width) for values in outputs)


def solution(mesh):
    rows = P(("grp", "sp"), None)
    return jax.shard_map(
        local,
        mesh=mesh,
        in_specs=(rows, rows, rows, rows, P(), P(), P("grp", None), P("grp", "sp", None)),
        out_specs=(rows, rows, rows, rows),
        check_vma=False,
    )
```

```python
import math

import jax
import jax.numpy as jnp
from jax import lax
from jax.experimental import pallas as pl
from jax.experimental.pallas import tpu as pltpu
from jax.sharding import PartitionSpec as P

HDIM = 128
TOK_FRAME = 64
SLAB = 8
WIDTH = 4096
S_GRP = 2048
FRAMES_GRP = 32
NVID = 4
MOSTF = 21
N_GRP = 16
N_SP = 16
BIG = MOSTF * TOK_FRAME
REST = S_GRP - BIG
PER_FRAME = TOK_FRAME // SLAB
PAIR = 2 * HDIM
PART = 8

EPSILON = 1e-06
MASKED = -1e30
SCALING = 1.0 / math.sqrt(HDIM)
LOG2E = math.log2(math.e)
MIB = 1 << 20
ATT_VMEM = 40 * MIB

BF16 = jnp.bfloat16
F32 = jnp.float32


def rms_factor(wide):
    return lax.rsqrt(jnp.mean(wide * wide, axis=-1, keepdims=True) + EPSILON)


def pack_kernel(
    dest,
    q_ref,
    k_ref,
    v_ref,
    c_ref,
    qg_hbm,
    kg_hbm,
    out_ref,
    factor_ref,
    held,
    qg_ref,
    kg_ref,
    arrived,
    ready,
):
    gains = (
        pltpu.make_async_copy(qg_hbm, qg_ref, ready.at[0]),
        pltpu.make_async_copy(kg_hbm, kg_ref, ready.at[1]),
    )
    def fetch(which, part):
        source = (q_ref, k_ref, v_ref, c_ref)[which]
        rows = pl.ds(part * PART, PART)
        return pltpu.make_async_copy(
            source.at[rows], held.at[which, rows], arrived.at[which, part]
        )

    for copy in gains:
        copy.start()
    for part in range(N_GRP // PART):
        for which in range(4):
            fetch(which, part).start()
    for copy in gains:
        copy.wait()

    def normalize(which, slab, gain_ref):
        wide = held[which, slab].astype(F32)
        factor = rms_factor(wide)
        factor_ref[which, slab] = jnp.broadcast_to(factor, (SLAB, HDIM))
        return (wide * factor * gain_ref[...]).astype(BF16)

    for part in range(N_GRP // PART):
        for which in range(4):
            fetch(which, part).wait()
        for slab in range(part * PART, (part + 1) * PART):
            rows = (
                normalize(0, slab, qg_ref),
                normalize(1, slab, kg_ref),
                held[2, slab],
                held[3, slab],
            )
            for owner in range(N_SP):
                for which in range(4):
                    piece = rows[which][:, owner * PAIR : (owner + 1) * PAIR]
                    out_ref[dest[slab], owner, which] = piece


def pack(dest, query_in, key_in, value_in, cot, query_gain, key_gain):
    smem = pl.BlockSpec(memory_space=pltpu.SMEM)
    vmem = pl.BlockSpec(memory_space=pltpu.VMEM)
    hbm = pl.BlockSpec(memory_space=pltpu.HBM)
    operands = [
        pltpu.with_memory_space_constraint(values, pltpu.HBM)
        for values in (dest, query_in, key_in, value_in, cot, query_gain, key_gain)
    ]
    return pl.pallas_call(
        pack_kernel,
        in_specs=[smem, hbm, hbm, hbm, hbm, hbm, hbm],
        out_specs=[vmem, vmem],
        out_shape=[
            jax.ShapeDtypeStruct((N_GRP, N_SP, 4, SLAB, PAIR), BF16),
            jax.ShapeDtypeStruct((2, N_GRP, SLAB, HDIM), F32),
        ],
        scratch_shapes=[
            pltpu.VMEM((4, N_GRP, SLAB, WIDTH), BF16),
            pltpu.VMEM((1, WIDTH), F32),
            pltpu.VMEM((1, WIDTH), F32),
            pltpu.SemaphoreType.DMA((4, N_GRP // PART)),
            pltpu.SemaphoreType.DMA((2,)),
        ],
        compiler_params=pltpu.CompilerParams(vmem_limit_bytes=32 * MIB),
        name="pack",
    )(*operands)


def attend(q, keys, values, c, same):
    rows = (((1,), (1,)), ((), ()))
    over_rows = (((0,), (0,)), ((), ()))
    scores = lax.dot_general(q, keys, rows, preferred_element_type=F32)
    if same is not None:
        scores = jnp.where(same, scores, MASKED)
    row_max = jnp.max(scores, axis=1, keepdims=True)
    grown = jnp.exp2((scores - row_max) * (SCALING * LOG2E))
    probs = grown * (1.0 / jnp.sum(grown, axis=1, keepdims=True))
    weights = probs.astype(BF16)
    attended = jnp.dot(weights, values, preferred_element_type=F32).astype(BF16)
    row_dot = jnp.sum(c.astype(F32) * attended.astype(F32), axis=1, keepdims=True)
    dweights = lax.dot_general(c, values, rows, preferred_element_type=F32)
    dscores = (probs * (dweights - row_dot)).astype(BF16)
    d_query = jnp.dot(dscores, keys, preferred_element_type=F32) * SCALING
    d_key = lax.dot_general(q, dscores, over_rows, preferred_element_type=F32) * SCALING
    d_value = lax.dot_general(c, weights, over_rows, preferred_element_type=F32)
    return attended, d_query, d_key.T, d_value.T


def attention_kernel(frames, x_ref, out_ref, *held):
    counts = [frames[v] for v in range(NVID)]
    starts = [jnp.int32(0)]
    for v in range(NVID - 1):
        starts.append(starts[-1] + counts[v])
    before = jnp.int32(0)
    for v in range(NVID):
        before = before + jnp.where(counts[v] == MOSTF, starts[v], 0)

    def frame_rows(frame):
        inside = jnp.logical_and(frame >= before, frame < before + MOSTF)
        outside = jnp.where(frame < before, frame + MOSTF, frame)
        slot = jnp.where(inside, frame - before, outside) * TOK_FRAME
        return pl.ds(pl.multiple_of(slot, TOK_FRAME), TOK_FRAME)

    def video_of(rest_index):
        position = rest_index + jnp.where(rest_index >= before * TOK_FRAME, BIG, 0)
        found = jnp.zeros_like(position)
        for v in range(1, NVID):
            found = found + (position >= starts[v] * TOK_FRAME).astype(jnp.int32)
        return found

    down = lax.broadcasted_iota(jnp.int32, (REST, 1), 0)
    across = lax.broadcasted_iota(jnp.int32, (1, REST), 1)
    same = video_of(down) == video_of(across)
    slots = [frame_rows(frame) for frame in range(FRAMES_GRP)]

    def slab_rows(frame):
        return slice((frame % 2) * PER_FRAME, (frame % 2 + 1) * PER_FRAME)

    for frame in range(FRAMES_GRP):
        for which in range(4):
            block = x_ref[slab_rows(frame), frame // 2, which].astype(F32)
            block = block.reshape(TOK_FRAME, PAIR).astype(BF16)
            for head in range(2):
                lanes = slice(head * HDIM, (head + 1) * HDIM)
                held[8 * head + which][slots[frame], :] = block[:, lanes]
    for head in range(2):
        ins, outs = held[8 * head : 8 * head + 4], held[8 * head + 4 : 8 * head + 8]
        for section, mask in ((slice(0, BIG), None), (slice(BIG, S_GRP), same)):
            results = attend(*(ref[section, :] for ref in ins), mask)
            for which in range(4):
                outs[which][section, :] = results[which].astype(F32)
    for frame in range(FRAMES_GRP):
        for which in range(4):
            pair = [held[8 * head + 4 + which][slots[frame], :] for head in range(2)]
            block = jnp.concatenate(pair, axis=1)
            block = block.reshape(PER_FRAME, SLAB, PAIR)
            out_ref[slab_rows(frame), frame // 2, which] = block.astype(BF16)


def attention(frames, received):
    kept = [pltpu.VMEM((S_GRP, HDIM), BF16)] * 4 + [pltpu.VMEM((S_GRP, HDIM), F32)] * 4
    held = kept + kept
    return pl.pallas_call(
        attention_kernel,
        in_specs=[
            pl.BlockSpec(memory_space=pltpu.SMEM),
            pl.BlockSpec(memory_space=pltpu.VMEM),
        ],
        out_specs=pl.BlockSpec(memory_space=pltpu.VMEM),
        out_shape=jax.ShapeDtypeStruct((N_GRP, N_SP, 4, SLAB, PAIR), BF16),
        scratch_shapes=held,
        compiler_params=pltpu.CompilerParams(vmem_limit_bytes=ATT_VMEM),
        name="attention",
    )(frames, received)


def finish_kernel(
    dest,
    x_ref,
    factor_ref,
    q_ref,
    k_ref,
    qg_ref,
    kg_ref,
    att_ref,
    gq_ref,
    gk_ref,
    gv_ref,
    held,
    gone,
):
    def store(which, part):
        target = (att_ref, gq_ref, gk_ref, gv_ref)[which]
        rows = pl.ds(part * PART, PART)
        return pltpu.make_async_copy(held.at[which, rows], target.at[rows], gone.at[which, part])

    def normalize_back(values, factor, gain_ref, upstream):
        wide = values.astype(F32)
        scaled = gain_ref[...] * upstream.astype(F32)
        inner = jnp.mean(wide * scaled, axis=-1, keepdims=True)
        return (factor * scaled - wide * (factor * factor * factor * inner)).astype(BF16)

    for part in range(N_GRP // PART):
        for which in (0, 3):
            for slab in range(part * PART, (part + 1) * PART):
                for owner in range(N_SP):
                    columns = slice(owner * PAIR, (owner + 1) * PAIR)
                    held[which, slab, :, columns] = x_ref[dest[slab], owner, which]
            store(which, part).start()
    for part in range(N_GRP // PART):
        for which, source, gain_ref in ((1, q_ref, qg_ref), (2, k_ref, kg_ref)):
            for slab in range(part * PART, (part + 1) * PART):
                pieces = [x_ref[dest[slab], owner, which] for owner in range(N_SP)]
                upstream = jnp.concatenate(pieces, axis=1)
                held[which, slab] = normalize_back(
                    source[slab], factor_ref[which - 1, slab][:, :1], gain_ref, upstream
                )
            store(which, part).start()
    for part in range(N_GRP // PART):
        for which in range(4):
            store(which, part).wait()


def finish(dest, returned, factors, query_in, key_in, query_gain, key_gain):
    smem = pl.BlockSpec(memory_space=pltpu.SMEM)
    vmem = pl.BlockSpec(memory_space=pltpu.VMEM)
    hbm = pl.BlockSpec(memory_space=pl.ANY)
    return pl.pallas_call(
        finish_kernel,
        in_specs=[smem, vmem, vmem, vmem, vmem, vmem, vmem],
        out_specs=[hbm, hbm, hbm, hbm],
        out_shape=[jax.ShapeDtypeStruct((N_GRP, SLAB, WIDTH), BF16)] * 4,
        scratch_shapes=[
            pltpu.VMEM((4, N_GRP, SLAB, WIDTH), BF16),
            pltpu.SemaphoreType.DMA((4, N_GRP // PART)),
        ],
        compiler_params=pltpu.CompilerParams(vmem_limit_bytes=32 * MIB),
        name="finish",
    )(dest, returned, factors, query_in, key_in, query_gain, key_gain)


def exchange(values):
    flat = values.reshape(N_GRP * N_SP, 4, SLAB, PAIR)
    moved = lax.all_to_all(flat, ("grp", "sp"), split_axis=0, concat_axis=0, tiled=True)
    return moved.reshape(values.shape)


def local(query_in, key_in, value_in, out_cotangent, query_gain, key_gain, frames, slab_group):
    tokens, width = query_in.shape
    dest = slab_group.reshape(N_GRP)

    def slabs(values):
        return values.reshape(N_GRP, SLAB, width)

    gains = (query_gain.reshape(1, width), key_gain.reshape(1, width))
    sent, factors = pack(
        dest, slabs(query_in), slabs(key_in), slabs(value_in), slabs(out_cotangent), *gains
    )
    results = attention(frames.reshape(NVID), exchange(sent))
    outputs = finish(dest, exchange(results), factors, slabs(query_in), slabs(key_in), *gains)
    return tuple(values.reshape(tokens, width) for values in outputs)


def solution(mesh):
    rows = P(("grp", "sp"), None)
    return jax.shard_map(
        local,
        mesh=mesh,
        in_specs=(rows, rows, rows, rows, P(), P(), P("grp", None), P("grp", "sp", None)),
        out_specs=(rows, rows, rows, rows),
        check_vma=False,
    )
```

```python
import math

import jax
import jax.numpy as jnp
from jax import lax
from jax.experimental import pallas as pl
from jax.experimental.pallas import tpu as pltpu
from jax.sharding import PartitionSpec as P

HDIM = 128
TOK_FRAME = 64
SLAB = 8
WIDTH = 4096
S_GRP = 2048
FRAMES_GRP = 32
NVID = 4
MOSTF = 21
N_GRP = 16
N_SP = 16
BIG = MOSTF * TOK_FRAME
REST = S_GRP - BIG
PER_FRAME = TOK_FRAME // SLAB
PAIR = 2 * HDIM
PART = 8
HOME_PART = 4

EPSILON = 1e-06
MASKED = -1e30
SCALING = 1.0 / math.sqrt(HDIM)
LOG2E = math.log2(math.e)
MIB = 1 << 20
ATT_VMEM = 40 * MIB

BF16 = jnp.bfloat16
F32 = jnp.float32


def rms_factor(wide):
    return lax.rsqrt(jnp.mean(wide * wide, axis=-1, keepdims=True) + EPSILON)


def pack_kernel(
    dest,
    q_ref,
    k_ref,
    v_ref,
    c_ref,
    qg_hbm,
    kg_hbm,
    out_ref,
    factor_ref,
    held,
    qg_ref,
    kg_ref,
    arrived,
    ready,
):
    gains = (
        pltpu.make_async_copy(qg_hbm, qg_ref, ready.at[0]),
        pltpu.make_async_copy(kg_hbm, kg_ref, ready.at[1]),
    )
    def fetch(which, part):
        source = (q_ref, k_ref, v_ref, c_ref)[which]
        rows = pl.ds(part * PART, PART)
        return pltpu.make_async_copy(
            source.at[rows], held.at[which, rows], arrived.at[which, part]
        )

    for part in range(N_GRP // PART):
        for which in range(4):
            fetch(which, part).start()
            if part == 0 and which < 2:
                gains[which].start()
    for copy in gains:
        copy.wait()

    def normalize(which, slab, gain_ref):
        wide = held[which, slab].astype(F32)
        factor = rms_factor(wide)
        factor_ref[which, slab] = jnp.broadcast_to(factor, (SLAB, HDIM))
        return (wide * factor * gain_ref[...]).astype(BF16)

    for part in range(N_GRP // PART):
        for which in range(4):
            fetch(which, part).wait()
        for slab in range(part * PART, (part + 1) * PART):
            rows = (
                normalize(0, slab, qg_ref),
                normalize(1, slab, kg_ref),
                held[2, slab],
                held[3, slab],
            )
            for owner in range(N_SP):
                for which in range(4):
                    piece = rows[which][:, owner * PAIR : (owner + 1) * PAIR]
                    out_ref[dest[slab], owner, which] = piece


def pack(dest, query_in, key_in, value_in, cot, query_gain, key_gain):
    smem = pl.BlockSpec(memory_space=pltpu.SMEM)
    vmem = pl.BlockSpec(memory_space=pltpu.VMEM)
    hbm = pl.BlockSpec(memory_space=pltpu.HBM)
    operands = [
        pltpu.with_memory_space_constraint(values, pltpu.HBM)
        for values in (dest, query_in, key_in, value_in, cot, query_gain, key_gain)
    ]
    return pl.pallas_call(
        pack_kernel,
        in_specs=[smem, hbm, hbm, hbm, hbm, hbm, hbm],
        out_specs=[vmem, vmem],
        out_shape=[
            jax.ShapeDtypeStruct((N_GRP, N_SP, 4, SLAB, PAIR), BF16),
            jax.ShapeDtypeStruct((2, N_GRP, SLAB, HDIM), F32),
        ],
        scratch_shapes=[
            pltpu.VMEM((4, N_GRP, SLAB, WIDTH), BF16),
            pltpu.VMEM((1, WIDTH), F32),
            pltpu.VMEM((1, WIDTH), F32),
            pltpu.SemaphoreType.DMA((4, N_GRP // PART)),
            pltpu.SemaphoreType.DMA((2,)),
        ],
        compiler_params=pltpu.CompilerParams(vmem_limit_bytes=32 * MIB),
        name="pack",
    )(*operands)


def attend(q, keys, values, c, same):
    rows = (((1,), (1,)), ((), ()))
    over_rows = (((0,), (0,)), ((), ()))
    scores = lax.dot_general(q, keys, rows, preferred_element_type=F32)
    if same is not None:
        scores = jnp.where(same, scores, MASKED)
    row_max = jnp.max(scores, axis=1, keepdims=True)
    grown = jnp.exp2((scores - row_max) * (SCALING * LOG2E))
    probs = grown * (1.0 / jnp.sum(grown, axis=1, keepdims=True))
    weights = probs.astype(BF16)
    attended = jnp.dot(weights, values, preferred_element_type=F32).astype(BF16)
    row_dot = jnp.sum(c.astype(F32) * attended.astype(F32), axis=1, keepdims=True)
    dweights = lax.dot_general(c, values, rows, preferred_element_type=F32)
    dscores = (probs * (dweights - row_dot)).astype(BF16)
    d_query = jnp.dot(dscores, keys, preferred_element_type=F32) * SCALING
    d_key = lax.dot_general(q, dscores, over_rows, preferred_element_type=F32) * SCALING
    d_value = lax.dot_general(c, weights, over_rows, preferred_element_type=F32)
    return attended, d_query, d_key.T, d_value.T


def attention_kernel(frames, x_ref, out_ref, *held):
    counts = [frames[v] for v in range(NVID)]
    starts = [jnp.int32(0)]
    for v in range(NVID - 1):
        starts.append(starts[-1] + counts[v])
    before = jnp.int32(0)
    for v in range(NVID):
        before = before + jnp.where(counts[v] == MOSTF, starts[v], 0)

    def frame_rows(frame):
        inside = jnp.logical_and(frame >= before, frame < before + MOSTF)
        outside = jnp.where(frame < before, frame + MOSTF, frame)
        slot = jnp.where(inside, frame - before, outside) * TOK_FRAME
        return pl.ds(pl.multiple_of(slot, TOK_FRAME), TOK_FRAME)

    def video_of(rest_index):
        position = rest_index + jnp.where(rest_index >= before * TOK_FRAME, BIG, 0)
        found = jnp.zeros_like(position)
        for v in range(1, NVID):
            found = found + (position >= starts[v] * TOK_FRAME).astype(jnp.int32)
        return found

    down = lax.broadcasted_iota(jnp.int32, (REST, 1), 0)
    across = lax.broadcasted_iota(jnp.int32, (1, REST), 1)
    same = video_of(down) == video_of(across)
    slots = [frame_rows(frame) for frame in range(FRAMES_GRP)]

    def slab_rows(frame):
        return slice((frame % 2) * PER_FRAME, (frame % 2 + 1) * PER_FRAME)

    for frame in range(FRAMES_GRP):
        for which in range(4):
            block = x_ref[slab_rows(frame), frame // 2, which].astype(F32)
            block = block.reshape(TOK_FRAME, PAIR).astype(BF16)
            for head in range(2):
                lanes = slice(head * HDIM, (head + 1) * HDIM)
                held[8 * head + which][slots[frame], :] = block[:, lanes]
    for head in range(2):
        ins, outs = held[8 * head : 8 * head + 4], held[8 * head + 4 : 8 * head + 8]
        for section, mask in ((slice(0, BIG), None), (slice(BIG, S_GRP), same)):
            results = attend(*(ref[section, :] for ref in ins), mask)
            for which in range(4):
                outs[which][section, :] = results[which].astype(F32)
    for frame in range(FRAMES_GRP):
        for which in range(4):
            pair = [held[8 * head + 4 + which][slots[frame], :] for head in range(2)]
            block = jnp.concatenate(pair, axis=1)
            block = block.reshape(PER_FRAME, SLAB, PAIR)
            out_ref[slab_rows(frame), frame // 2, which] = block.astype(BF16)


def attention(frames, received):
    kept = [pltpu.VMEM((S_GRP, HDIM), BF16)] * 4 + [pltpu.VMEM((S_GRP, HDIM), F32)] * 4
    held = kept + kept
    return pl.pallas_call(
        attention_kernel,
        in_specs=[
            pl.BlockSpec(memory_space=pltpu.SMEM),
            pl.BlockSpec(memory_space=pltpu.VMEM),
        ],
        out_specs=pl.BlockSpec(memory_space=pltpu.VMEM),
        out_shape=jax.ShapeDtypeStruct((N_GRP, N_SP, 4, SLAB, PAIR), BF16),
        scratch_shapes=held,
        compiler_params=pltpu.CompilerParams(vmem_limit_bytes=ATT_VMEM),
        name="attention",
    )(frames, received)


def finish_kernel(
    dest,
    x_ref,
    factor_ref,
    q_ref,
    k_ref,
    qg_ref,
    kg_ref,
    att_ref,
    gq_ref,
    gk_ref,
    gv_ref,
    held,
    gone,
):
    def store(which, part):
        target = (att_ref, gq_ref, gk_ref, gv_ref)[which]
        rows = pl.ds(part * HOME_PART, HOME_PART)
        return pltpu.make_async_copy(held.at[which, rows], target.at[rows], gone.at[which, part])

    def normalize_back(values, factor, gain_ref, upstream):
        wide = values.astype(F32)
        scaled = gain_ref[...] * upstream.astype(F32)
        inner = jnp.mean(wide * scaled, axis=-1, keepdims=True)
        return (factor * scaled - wide * (factor * factor * factor * inner)).astype(BF16)

    for part in range(N_GRP // HOME_PART):
        for which in (0, 3):
            for slab in range(part * HOME_PART, (part + 1) * HOME_PART):
                for owner in range(N_SP):
                    columns = slice(owner * PAIR, (owner + 1) * PAIR)
                    held[which, slab, :, columns] = x_ref[dest[slab], owner, which]
            store(which, part).start()
    for part in range(N_GRP // HOME_PART):
        for which, source, gain_ref in ((1, q_ref, qg_ref), (2, k_ref, kg_ref)):
            for slab in range(part * HOME_PART, (part + 1) * HOME_PART):
                pieces = [x_ref[dest[slab], owner, which] for owner in range(N_SP)]
                upstream = jnp.concatenate(pieces, axis=1)
                held[which, slab] = normalize_back(
                    source[slab], factor_ref[which - 1, slab][:, :1], gain_ref, upstream
                )
            store(which, part).start()
    for part in range(N_GRP // HOME_PART):
        for which in range(4):
            store(which, part).wait()


def finish(dest, returned, factors, query_in, key_in, query_gain, key_gain):
    smem = pl.BlockSpec(memory_space=pltpu.SMEM)
    vmem = pl.BlockSpec(memory_space=pltpu.VMEM)
    hbm = pl.BlockSpec(memory_space=pl.ANY)
    return pl.pallas_call(
        finish_kernel,
        in_specs=[smem, vmem, vmem, vmem, vmem, vmem, vmem],
        out_specs=[hbm, hbm, hbm, hbm],
        out_shape=[jax.ShapeDtypeStruct((N_GRP, SLAB, WIDTH), BF16)] * 4,
        scratch_shapes=[
            pltpu.VMEM((4, N_GRP, SLAB, WIDTH), BF16),
            pltpu.SemaphoreType.DMA((4, N_GRP // HOME_PART)),
        ],
        compiler_params=pltpu.CompilerParams(vmem_limit_bytes=32 * MIB),
        name="finish",
    )(dest, returned, factors, query_in, key_in, query_gain, key_gain)


def exchange(values):
    flat = values.reshape(N_GRP * N_SP, 4, SLAB, PAIR)
    moved = lax.all_to_all(flat, ("grp", "sp"), split_axis=0, concat_axis=0, tiled=True)
    return moved.reshape(values.shape)


def local(query_in, key_in, value_in, out_cotangent, query_gain, key_gain, frames, slab_group):
    tokens, width = query_in.shape
    dest = slab_group.reshape(N_GRP)

    def slabs(values):
        return values.reshape(N_GRP, SLAB, width)

    gains = (query_gain.reshape(1, width), key_gain.reshape(1, width))
    sent, factors = pack(
        dest, slabs(query_in), slabs(key_in), slabs(value_in), slabs(out_cotangent), *gains
    )
    results = attention(frames.reshape(NVID), exchange(sent))
    outputs = finish(dest, exchange(results), factors, slabs(query_in), slabs(key_in), *gains)
    return tuple(values.reshape(tokens, width) for values in outputs)


def solution(mesh):
    rows = P(("grp", "sp"), None)
    return jax.shard_map(
        local,
        mesh=mesh,
        in_specs=(rows, rows, rows, rows, P(), P(), P("grp", None), P("grp", "sp", None)),
        out_specs=(rows, rows, rows, rows),
        check_vma=False,
    )
```
